32 devices in a mesh: groups: 2 (over x), expert: 8 (over z, y), narrow: 2 (over core).
Axes of the slice: x: 2, y: 2, z: 4, core: 2. Of those that a mesh axis runs over, the one named last changes fastest.
Arguments:
- tokens: bfloat16 [128, 5120], P(('groups', 'expert', 'narrow')), parts along dimension 0, may hold values from -6 to 6
- expert_ids: int32 [128], P(('groups', 'expert', 'narrow')), parts along dimension 0, may hold values from 0 to 2, as said below
- replica_plan: int32 [128], P(('groups', 'expert', 'narrow')), parts along dimension 0, may hold values from 0 to 1, as said below
- route_gate: bfloat16 [128], P(('groups', 'expert', 'narrow')), parts along dimension 0, may hold values from 0.099609375 to 1
- capacity: int32 [4], P(('groups', 'narrow')), parts along dimension 0, may hold values from 16 to 32, as said below
- cold_gate_up: bfloat16 [2, 5120, 2, 4096], P('narrow', None, None, 'expert'), may hold values from -0.078125 to 0.078125
- cold_down: bfloat16 [2, 4096, 5120], P('narrow', 'expert'), may hold values from -0.09375 to 0.09375
- hot_gate_up: bfloat16 [5120, 2, 4096], P(None, None, 'expert'), may hold values from -0.078125 to 0.078125
- hot_down: bfloat16 [4096, 5120], P('expert'), may hold values from -0.09375 to 0.09375
- shared_gate_up: bfloat16 [5120, 2, 8192], P(None, None, ('expert', 'narrow')), may hold values from -0.078125 to 0.078125
- shared_down: bfloat16 [8192, 5120], P(('expert', 'narrow')), may hold values from -0.0625 to 0.0625
Outputs:
- mixed: bfloat16 [128, 5120], P(('groups', 'expert', 'narrow')), parts along dimension 0
The draws below stay inside these ranges and needn't reach their ends.
There are 2 independent parts, one for each index of `groups`. The reference program is written for one: setup_inputs(seed, part) draws one part's arguments, and reference() takes and returns one part's arrays. A program takes and returns all parts, laid end to end along the dimension named above; an argument that names none is the same for every part. Nothing has to cross between parts.
Inputs may be any that keep to these rules, and one draw needn't show every extreme that they name: `expert_ids`: the value 2 names the replicated expert; of one device's tokens at most 3 have the same dest, and every device has a dest with exactly 3. `replica_plan`: read only for tokens of expert 2. `capacity`: some instance has exactly 32, and 32 or more tokens have it as dest.
All inputs are finite; a program needn't handle non-finite values.
Results may differ from the reference program's by a relative error of at most 0.0048.
Values may be sent and summed in bfloat16 or wider, within the bound.
No kernel may reach another device: no remote copies, remote signals or barrier semaphores. Data moves between devices by JAX's collectives and lax.ppermute only.
A program may use at most 192 MiB of HBM per device.

```python
import jax
import jax.numpy as jnp
from jax import lax

D = 5120
FR = 4096
SH = 8192
TOK = 4
SEND = 3
INST = 2
TOKENS = 64
CAP = 32


def routing_layout(key):
    blocks = TOKENS // TOK
    places = INST * SEND
    popular = jax.random.randint(jax.random.fold_in(key, 11), (INST,), 0, 4)
    noise = jax.random.randint(jax.random.fold_in(key, 12), (blocks, places), 0, 8)
    favored = jax.random.randint(jax.random.fold_in(key, 13), (blocks,), 0, INST)
    place_dest = jnp.arange(places, dtype=jnp.int32) // SEND
    score = popular[place_dest][None, :] + noise + 100 * (place_dest[None, :] == favored[:, None]).astype(jnp.int32)
    distinct = score * places + jnp.arange(places, dtype=jnp.int32)[None, :]
    chosen_scores, chosen = lax.top_k(distinct, TOK)
    shuffle = jax.random.randint(jax.random.fold_in(key, 14), (blocks, TOK), 0, 1024)
    order = jnp.argsort(shuffle * TOK + jnp.arange(TOK, dtype=jnp.int32)[None, :], axis=1)
    chosen = jnp.take_along_axis(chosen, order, axis=1)
    dest = (chosen // SEND).reshape(TOKENS).astype(jnp.int32)
    hot = jax.random.randint(jax.random.fold_in(key, 15), (TOKENS,), 0, 4) == 0
    return (dest, hot)


def draw_expert_ids(key, part):
    dest, hot = routing_layout(key)
    return jnp.where(hot, INST, dest).astype(jnp.int32)


def draw_replica_plan(key, part):
    dest, hot = routing_layout(key)
    key = jax.random.fold_in(key, 2)
    other = jax.random.randint(key, (TOKENS,), 0, INST)
    return jnp.where(hot, dest, other).astype(jnp.int32)


def draw_capacity(key, part):
    dest, hot = routing_layout(key)
    key = jax.random.fold_in(key, 3)
    loads = jnp.sum((dest[:, None] == jnp.arange(INST, dtype=jnp.int32)[None, :]).astype(jnp.int32), axis=0)
    fullest = jnp.argmax(loads)
    values = jax.random.randint(key, (INST,), CAP // 2, CAP + 1)
    return jnp.where(jnp.arange(INST) == fullest, CAP, values).astype(jnp.int32)


def steps_of(own_key, extent, shards, smallest, top_value):
    loudness, own = 1.0, jax.random.fold_in(own_key, 6)
    for position, parts in shards:
        heights = jnp.exp(jax.random.uniform(jax.random.fold_in(own, position), (parts,), jnp.float32, smallest / len(shards), top_value / len(shards)))
        loudness = loudness * jnp.repeat(heights, extent[position] // parts).reshape([-1 if axis == position else 1 for axis in range(len(extent))])
    return loudness


def bell_draw(stream_key, shape, scale, limit, shards=(), kind=jnp.bfloat16):
    loudness = steps_of(stream_key, shape, shards, -0.22, 0.18) if shards else 1.0
    result = jax.random.normal(stream_key, shape, jnp.float32) * scale * loudness
    return jnp.minimum(jnp.maximum(result, -limit), limit).astype(kind)


def setup_inputs(seed: int = 0, part: int = 0) -> dict:
    splits = jax.random.split(jax.random.key(seed), 12)
    own_keys = jax.random.split(jax.random.fold_in(splits[11], part), 12)
    tokens = bell_draw(own_keys[0], (TOKENS, D), 1.0, 6.0, ((0, 16),))
    expert_ids = draw_expert_ids(jax.random.fold_in(jax.random.fold_in(splits[11], part), 71), part)
    replica_plan = draw_replica_plan(jax.random.fold_in(jax.random.fold_in(splits[11], part), 71), part)
    route_gate = jnp.clip(0.099609375 + 0.9003906 * jax.random.uniform(own_keys[3], (TOKENS,), jnp.float32) ** steps_of(own_keys[3], (TOKENS,), ((0, 16),), -0.2, 0.2), 0.099609375, 1.0).astype(jnp.bfloat16)
    capacity = draw_capacity(jax.random.fold_in(jax.random.fold_in(splits[11], part), 71), part)
    cold_gate_up = bell_draw(splits[5], (INST, D, 2, FR), D ** -0.5, 0.078125, ((0, 2), (3, 8)))
    cold_down = bell_draw(splits[6], (INST, FR, D), FR ** -0.5, 0.09375, ((0, 2), (1, 8)))
    hot_gate_up = bell_draw(splits[7], (D, 2, FR), D ** -0.5, 0.078125, ((2, 8),))
    hot_down = bell_draw(splits[8], (FR, D), FR ** -0.5, 0.09375, ((0, 8),))
    shared_gate_up = bell_draw(splits[9], (D, 2, SH), D ** -0.5, 0.078125, ((2, 16),))
    shared_down = bell_draw(splits[10], (SH, D), SH ** -0.5, 0.0625, ((0, 16),))
    return dict(tokens=tokens, expert_ids=expert_ids, replica_plan=replica_plan, route_gate=route_gate, capacity=capacity, cold_gate_up=cold_gate_up, cold_down=cold_down, hot_gate_up=hot_gate_up, hot_down=hot_down, shared_gate_up=shared_gate_up, shared_down=shared_down)


def expert_rows(rows, gate_up, down):
    width = down.shape[0]
    mixed_in = jnp.dot(rows, gate_up, preferred_element_type=jnp.float32)
    hidden = (jax.nn.silu(mixed_in[:, :width]) * mixed_in[:, width:]).astype(jnp.bfloat16)
    return jnp.dot(hidden, down, preferred_element_type=jnp.float32)


def reference(tokens, expert_ids, replica_plan, route_gate, capacity, cold_gate_up, cold_down, hot_gate_up, hot_down, shared_gate_up, shared_down):
    hot = expert_ids == INST
    dest = jnp.where(hot, replica_plan, expert_ids).astype(jnp.int32)
    onehot = (dest[:, None] == jnp.arange(INST, dtype=jnp.int32)[None, :]).astype(jnp.int32)
    rank = jnp.sum((jnp.cumsum(onehot, axis=0) - 1) * onehot, axis=1)
    kept = rank < capacity[dest]
    padded = jnp.concatenate([tokens, jnp.zeros((1, D), jnp.bfloat16)], axis=0)
    hot_padded = jnp.concatenate([hot, jnp.zeros((1,), bool)], axis=0)
    warm_weight = hot_gate_up.reshape(D, 2 * FR)

    def per_instance(index):
        chosen = kept & (dest == index)
        picked = jnp.nonzero(chosen, size=CAP, fill_value=TOKENS)[0].astype(jnp.int32)
        rows = padded[picked]
        cold = expert_rows(rows, cold_gate_up[index].reshape(D, 2 * FR), cold_down[index])
        warm = expert_rows(rows, warm_weight, hot_down)
        return picked, jnp.where(hot_padded[picked][:, None], warm, cold)

    picked, results = lax.map(per_instance, jnp.arange(INST, dtype=jnp.int32))
    routed = jnp.zeros((TOKENS + 1, D), jnp.float32).at[picked.reshape(-1)].set(results.reshape(-1, D))
    routed = routed[:TOKENS]
    shared_in = jnp.dot(tokens, shared_gate_up.reshape(D, 2 * SH), preferred_element_type=jnp.float32)
    shared_hidden = (jax.nn.silu(shared_in[:, :SH]) * shared_in[:, SH:]).astype(jnp.bfloat16)
    shared = jnp.dot(shared_hidden, shared_down, preferred_element_type=jnp.float32)
    return (shared + route_gate.astype(jnp.float32)[:, None] * routed).astype(jnp.bfloat16)
```

```python
import functools

import jax
import jax.numpy as jnp
from jax import lax
from jax.experimental import pallas as pl
from jax.experimental.pallas import tpu as pltpu
from jax.sharding import PartitionSpec as P

META = 128
LANE = 128
STEP = 512
DOWN_CHUNK = 1280


def expert_swap(x, bits):
    size = lax.axis_size("expert")
    return lax.ppermute(x, "expert", [(i, i ^ bits) for i in range(size)])


def narrow_swap(x):
    return lax.ppermute(x, "narrow", [(0, 1), (1, 0)])


def token_index(row, tok_rows, outer, expert, narrow):
    block = row // tok_rows
    other_narrow = block // outer
    other_low = (block % outer) // (outer // 2)
    other_high = block % (outer // 2)
    from_expert = expert ^ (2 * other_high + other_low)
    from_narrow = narrow ^ other_narrow
    return (from_expert * 2 + from_narrow) * tok_rows + row % tok_rows


def layer_kernel(
    split_hot,
    tok_rows,
    outer,
    here_ref,
    far_ref,
    shared_in_ref,
    cold_in_ref,
    hot_in_ref,
    shared_out_ref,
    cold_out_ref,
    hot_out_ref,
    mine_ref,
    other_ref,
    x_ref,
    spread_ref,
    shared_in,
    cold_in,
    hot_in,
    shared_out,
    cold_out,
    hot_out,
    in_sems,
    out_sems,
):
    width = shared_in_ref.shape[0]
    narrow = lax.axis_index("narrow")
    expert = lax.axis_index("expert")
    half = here_ref.shape[0]
    rows = 2 * half
    hot_cols = hot_in.shape[0] * LANE

    copies = {}
    for which, (source, target) in enumerate(
        (
            (shared_in_ref, shared_in),
            (cold_in_ref.at[0], cold_in),
            (hot_in_ref, hot_in),
        )
    ):
        flat = source.reshape(2 * width, source.shape[2])
        base = narrow * hot_cols if (which == 2 and split_hot) else 0
        for tile in range(target.shape[0]):
            start = base + tile * LANE
            if not isinstance(start, int):
                start = pl.multiple_of(start, LANE)
            copies["in", which, tile] = pltpu.make_async_copy(
                flat.at[:, pl.ds(start, LANE)], target.at[tile], in_sems.at[which, tile]
            )
    chunks = width // DOWN_CHUNK
    for chunk in range(chunks):
        columns = pl.ds(chunk * DOWN_CHUNK, DOWN_CHUNK)
        for which, (source, target) in enumerate(
            ((shared_out_ref, shared_out), (cold_out_ref.at[0], cold_out), (hot_out_ref, hot_out))
        ):
            taken = source.at[:, columns]
            if which == 2 and split_hot:
                taken = source.at[pl.ds(pl.multiple_of(narrow * hot_cols, LANE), hot_cols), columns]
            copies["out", which, chunk] = pltpu.make_async_copy(
                taken, target.at[:, columns], out_sems.at[which, chunk]
            )
    for copy in copies.values():
        copy.start()

    x_ref[pl.ds(0, half)] = here_ref[...]
    x_ref[pl.ds(half, half)] = far_ref[...]

    meta = x_ref[:, pl.ds(width, META)].astype(jnp.float32)
    ids, plan, gate = meta[:, 0:1], meta[:, 1:2], meta[:, 2:3]
    hot = ids == 2.0
    dest = jnp.where(hot, plan, ids)
    index_of = functools.partial(
        token_index, tok_rows=tok_rows, outer=outer, expert=expert, narrow=narrow
    )
    column_index = index_of(lax.broadcasted_iota(jnp.int32, (rows, rows), 0))
    row_index = index_of(lax.broadcasted_iota(jnp.int32, (rows, rows), 1))
    before = (row_index < column_index).astype(jnp.float32).astype(jnp.bfloat16)
    lane = lax.broadcasted_iota(jnp.int32, (rows, META), 1).astype(jnp.float32)
    onehot = (lane == dest).astype(jnp.float32)
    counts = jnp.dot(before, onehot.astype(jnp.bfloat16), preferred_element_type=jnp.float32)
    rank = jnp.sum(onehot * counts, axis=1, keepdims=True)
    at_home = dest == narrow.astype(jnp.float32)
    limit = jnp.where(at_home, meta[0:1, 3:4], meta[half : half + 1, 3:4])
    kept = rank < limit
    cold_rows = kept & at_home & jnp.logical_not(hot)
    hot_rows = kept & hot
    if not split_hot:
        hot_rows = hot_rows & at_home

    source_lane = lax.broadcasted_iota(jnp.int32, (LANE, 4 * LANE), 0)
    target_lane = lax.broadcasted_iota(jnp.int32, (LANE, 4 * LANE), 1)
    aim = jnp.where(target_lane < 2 * LANE, 2 * source_lane, 2 * source_lane + 1 + 2 * LANE)
    spread = (target_lane == aim).astype(jnp.float32).astype(jnp.bfloat16)
    for block in range(width // LANE):
        wide = jnp.dot(
            x_ref[:, pl.ds(block * LANE, LANE)], spread, preferred_element_type=jnp.float32
        ).astype(jnp.bfloat16)
        columns = pl.ds(block * 2 * LANE, 2 * LANE)
        spread_ref[pl.ds(0, rows), columns] = wide[:, : 2 * LANE]
        spread_ref[pl.ds(rows, rows), columns] = wide[:, 2 * LANE :]

    def hidden(which, weights, keep):
        tiles = weights.shape[0]
        for tile in range(tiles):
            copies["in", which, tile].wait()
        parts = []
        group = 2 if tiles % 2 == 0 else 1
        for first in range(0, tiles, group):
            total = jnp.zeros((2 * rows, group * LANE), jnp.float32)
            for step in range(2 * width // (2 * STEP)):
                depth = pl.ds(step * 2 * STEP, 2 * STEP)
                block = weights[first, depth, :]
                if group == 2:
                    block = jnp.concatenate([block, weights[first + 1, depth, :]], axis=1)
                total = total + jnp.dot(
                    spread_ref[:, depth], block, preferred_element_type=jnp.float32
                )
            value = jax.nn.silu(total[:rows]) * total[rows:]
            if keep is not None:
                value = jnp.where(keep, value, 0.0)
            parts.append(value.astype(jnp.bfloat16))
        return parts[0] if len(parts) == 1 else jnp.concatenate(parts, axis=1)

    shared_hidden = hidden(0, shared_in, None)
    cold_hidden = hidden(1, cold_in, cold_rows)
    hot_hidden = hidden(2, hot_in, hot_rows)
    for chunk in range(chunks):
        columns = pl.ds(chunk * DOWN_CHUNK, DOWN_CHUNK)
        for which in range(3):
            copies["out", which, chunk].wait()
        routed = jnp.dot(cold_hidden, cold_out[:, columns], preferred_element_type=jnp.float32)
        routed = routed + jnp.dot(
            hot_hidden, hot_out[:, columns], preferred_element_type=jnp.float32
        )
        total = gate * routed + jnp.dot(
            shared_hidden, shared_out[:, columns], preferred_element_type=jnp.float32
        )
        mine_ref[:, columns] = total[:half]
        other_ref[:, columns] = total[half:].astype(jnp.bfloat16)


def layer(here, far, weights, tok_rows):
    shared_in, cold_in, hot_in, shared_out, cold_out, hot_out = weights
    outer = lax.axis_size("expert")
    width, _, part = shared_in.shape
    cold_part = cold_in.shape[3]
    hot_part = hot_in.shape[2]
    split_hot = hot_part % (2 * LANE) == 0
    hot_used = hot_part // 2 if split_hot else hot_part
    half = here.shape[0]
    kernel = functools.partial(layer_kernel, split_hot, tok_rows, outer)
    tiles = max(part, cold_part, hot_used) // LANE
    in_vmem = pl.BlockSpec(memory_space=pltpu.VMEM)
    anywhere = pl.BlockSpec(memory_space=pl.ANY)
    return pl.pallas_call(
        kernel,
        out_shape=(
            jax.ShapeDtypeStruct((half, width), jnp.float32),
            jax.ShapeDtypeStruct((half, width), jnp.bfloat16),
        ),
        in_specs=[in_vmem, in_vmem] + [anywhere] * 6,
        out_specs=(in_vmem, in_vmem),
        scratch_shapes=[
            pltpu.VMEM((2 * half, width + META), jnp.bfloat16),
            pltpu.VMEM((4 * half, 2 * width), jnp.bfloat16),
            pltpu.VMEM((part // LANE, 2 * width, LANE), jnp.bfloat16),
            pltpu.VMEM((cold_part // LANE, 2 * width, LANE), jnp.bfloat16),
            pltpu.VMEM((hot_used // LANE, 2 * width, LANE), jnp.bfloat16),
            pltpu.VMEM((part, width), jnp.bfloat16),
            pltpu.VMEM((cold_part, width), jnp.bfloat16),
            pltpu.VMEM((hot_used, width), jnp.bfloat16),
            pltpu.SemaphoreType.DMA((3, tiles)),
            pltpu.SemaphoreType.DMA((3, width // DOWN_CHUNK)),
        ],
        compiler_params=pltpu.CompilerParams(vmem_limit_bytes=56 << 20),
        name="layer",
    )(here, far, *weights)


def body(
    tokens,
    expert_ids,
    replica_plan,
    route_gate,
    capacity,
    cold_gate_up,
    cold_down,
    hot_gate_up,
    hot_down,
    shared_gate_up,
    shared_down,
):
    tok_rows, width = tokens.shape
    outer = lax.axis_size("expert")
    high = outer // 2
    lane = jnp.arange(META, dtype=jnp.int32)[None, :]
    meta = jnp.where(lane == 0, expert_ids.astype(jnp.bfloat16)[:, None], jnp.bfloat16(0))
    meta = jnp.where(lane == 1, replica_plan.astype(jnp.bfloat16)[:, None], meta)
    meta = jnp.where(lane == 2, route_gate[:, None], meta)
    meta = jnp.where(lane == 3, capacity.astype(jnp.bfloat16)[:, None], meta)
    packed = jnp.concatenate([tokens, meta], axis=1)
    line = jnp.concatenate(
        [packed] + [expert_swap(packed, 2 * step) for step in range(1, high)], axis=0
    )
    here = jnp.concatenate([line, expert_swap(line, 1)], axis=0)
    far = narrow_swap(here)
    weights = (shared_gate_up, cold_gate_up, hot_gate_up, shared_down, cold_down, hot_down)
    mine, other = layer(here, far, weights, tok_rows)
    mine = mine + narrow_swap(other).astype(jnp.float32)
    part = tok_rows * high
    mine = mine[:part] + expert_swap(mine[part:].astype(jnp.bfloat16), 1).astype(jnp.float32)
    total = mine[:tok_rows]
    for step in range(1, high):
        block = mine[step * tok_rows : (step + 1) * tok_rows].astype(jnp.bfloat16)
        total = total + expert_swap(block, 2 * step).astype(jnp.float32)
    return total.astype(jnp.bfloat16)


def solution(mesh):
    in_specs = (
        P(("groups", "expert", "narrow"), None),
        P(("groups", "expert", "narrow")),
        P(("groups", "expert", "narrow")),
        P(("groups", "expert", "narrow")),
        P(("groups", "narrow")),
        P("narrow", None, None, "expert"),
        P("narrow", "expert", None),
        P(None, None, "expert"),
        P("expert", None),
        P(None, None, ("expert", "narrow")),
        P(("expert", "narrow"), None),
    )
    out_specs = P(("groups", "expert", "narrow"), None)
    return jax.shard_map(body, mesh=mesh, in_specs=in_specs, out_specs=out_specs, check_vma=False)
```

```python
import functools

import jax
import jax.numpy as jnp
from jax import lax
from jax.experimental import pallas as pl
from jax.experimental.pallas import tpu as pltpu
from jax.sharding import PartitionSpec as P

META = 128
LANE = 128
STEP = 512
DOWN_CHUNK = 2560


def expert_swap(x, bits):
    size = lax.axis_size("expert")
    return lax.ppermute(x, "expert", [(i, i ^ bits) for i in range(size)])


def narrow_swap(x):
    return lax.ppermute(x, "narrow", [(0, 1), (1, 0)])


def token_index(row, tok_rows, outer, expert, narrow):
    block = row // tok_rows
    other_narrow = block // outer
    other_low = (block % outer) // (outer // 2)
    other_high = block % (outer // 2)
    from_expert = expert ^ (2 * other_high + other_low)
    from_narrow = narrow ^ other_narrow
    return (from_expert * 2 + from_narrow) * tok_rows + row % tok_rows


def pack_kernel(tokens_ref, ids_ref, plan_ref, gate_ref, capacity_ref, packed_ref):
    rows, width = tokens_ref.shape
    packed_ref[:, pl.ds(0, width)] = tokens_ref[...]
    own = lax.broadcasted_iota(jnp.int32, (rows, rows), 0) == lax.broadcasted_iota(
        jnp.int32, (rows, rows), 1
    )

    def per_row(ref):
        spread = jnp.broadcast_to(ref[...].astype(jnp.float32), (rows, rows))
        return jnp.sum(jnp.where(own, spread, 0.0), axis=1, keepdims=True)

    lane = lax.broadcasted_iota(jnp.int32, (rows, META), 1)
    meta = jnp.where(lane == 0, per_row(ids_ref), 0.0)
    meta = jnp.where(lane == 1, per_row(plan_ref), meta)
    meta = jnp.where(lane == 2, per_row(gate_ref), meta)
    meta = jnp.where(lane == 3, capacity_ref[...].astype(jnp.float32), meta)
    packed_ref[:, pl.ds(width, META)] = meta.astype(jnp.bfloat16)


def pack(tokens, ids, plan, gate, capacity):
    rows, width = tokens.shape
    return pl.pallas_call(
        pack_kernel,
        out_shape=pltpu.VMEM((rows, width + META), jnp.bfloat16),
        in_specs=[pl.BlockSpec(memory_space=pltpu.VMEM)] * 5,
        out_specs=pl.BlockSpec(memory_space=pltpu.VMEM),
        name="pack",
    )(tokens, *(v.reshape(1, -1) for v in (ids, plan, gate, capacity)))


def tile_copies(source, target, sems, base):
    width = source.shape[0]
    flat = source.reshape(2 * width, source.shape[2])
    copies = []
    for tile in range(target.shape[0]):
        start = base + tile * LANE
        if not isinstance(start, int):
            start = pl.multiple_of(start, LANE)
        copies.append(
            pltpu.make_async_copy(
                flat.at[:, pl.ds(start, LANE)], target.at[tile], sems.at[tile]
            )
        )
    return copies


def spread_rows(x_ref, spread_ref, width):
    rows = x_ref.shape[0]
    source_lane = lax.broadcasted_iota(jnp.int32, (LANE, 4 * LANE), 0)
    target_lane = lax.broadcasted_iota(jnp.int32, (LANE, 4 * LANE), 1)
    aim = jnp.where(target_lane < 2 * LANE, 2 * source_lane, 2 * source_lane + 1 + 2 * LANE)
    spread = (target_lane == aim).astype(jnp.float32).astype(jnp.bfloat16)
    for block in range(width // LANE):
        wide = jnp.dot(
            x_ref[:, pl.ds(block * LANE, LANE)], spread, preferred_element_type=jnp.float32
        ).astype(jnp.bfloat16)
        columns = pl.ds(block * 2 * LANE, 2 * LANE)
        spread_ref[pl.ds(0, rows), columns] = wide[:, : 2 * LANE]
        spread_ref[pl.ds(rows, rows), columns] = wide[:, 2 * LANE :]


def fetch_kernel(source_ref, after_ref, target_ref, done_ref, sems):
    del after_ref
    source = source_ref if len(source_ref.shape) == 3 else source_ref.at[0]
    copies = tile_copies(source, target_ref, sems, 0)
    for copy in copies:
        copy.start()
    for copy in copies:
        copy.wait()
    done_ref[...] = jnp.zeros_like(done_ref)


def join_kernel(*refs):
    pieces, joined_ref = refs[1:-1], refs[-1]
    joined_ref[...] = jnp.concatenate(
        [piece[...].astype(jnp.float32) for piece in pieces], axis=0
    ).astype(joined_ref.dtype)


def join(after, pieces):
    rows, width = pieces[0].shape
    in_vmem = pl.BlockSpec(memory_space=pltpu.VMEM)
    return pl.pallas_call(
        join_kernel,
        out_shape=pltpu.VMEM((len(pieces) * rows, width), pieces[0].dtype),
        in_specs=[in_vmem] * (1 + len(pieces)),
        out_specs=in_vmem,
        compiler_params=pltpu.CompilerParams(vmem_limit_bytes=4 << 20),
        name="join",
    )(after, *pieces)


def fetch(source, after):
    width, _, part = source.shape[-3:]
    size = source.size * source.dtype.itemsize
    return pl.pallas_call(
        fetch_kernel,
        out_shape=(
            pltpu.VMEM((part // LANE, 2 * width, LANE), jnp.bfloat16),
            pltpu.VMEM((8, LANE), jnp.float32),
        ),
        in_specs=[pl.BlockSpec(memory_space=pltpu.HBM), pl.BlockSpec(memory_space=pltpu.VMEM)],
        out_specs=(pl.BlockSpec(memory_space=pltpu.VMEM),) * 2,
        scratch_shapes=[pltpu.SemaphoreType.DMA((part // LANE,))],
        cost_estimate=pl.CostEstimate(flops=0, bytes_accessed=2 * size, transcendentals=0),
        compiler_params=pltpu.CompilerParams(vmem_limit_bytes=4 << 20),
        name="fetch",
    )(pltpu.with_memory_space_constraint(source, pltpu.HBM), after)


def near_spread_kernel(here_ref, spread_ref):
    spread_rows(here_ref, spread_ref, spread_ref.shape[1] // 2)


def spread_near(here):
    half, width = here.shape[0], here.shape[1] - META
    in_vmem = pl.BlockSpec(memory_space=pltpu.VMEM)
    return pl.pallas_call(
        near_spread_kernel,
        out_shape=pltpu.VMEM((2 * half, 2 * width), jnp.bfloat16),
        in_specs=[in_vmem],
        out_specs=in_vmem,
        compiler_params=pltpu.CompilerParams(vmem_limit_bytes=4 << 20),
        name="spread",
    )(here)


def layer_kernel(
    split_hot,
    tok_rows,
    outer,
    here_ref,
    far_ref,
    near_spread_ref,
    shared_in,
    cold_in,
    hot_in_ref,
    shared_out,
    cold_out,
    hot_out_ref,
    mine_ref,
    other_ref,
    far_spread_ref,
    hot_in,
    hot_out,
    in_sems,
    out_sem,
    hid_ref,
):
    width = mine_ref.shape[1]
    narrow = lax.axis_index("narrow")
    expert = lax.axis_index("expert")
    half = here_ref.shape[0]
    rows = 2 * half
    hot_used = hot_out.shape[0]
    base = narrow * hot_used if split_hot else 0
    in_copies = tile_copies(hot_in_ref, hot_in, in_sems, base)
    taken = hot_out_ref
    if split_hot:
        taken = hot_out_ref.at[pl.ds(pl.multiple_of(base, LANE), hot_used)]
    out_copy = pltpu.make_async_copy(taken, hot_out, out_sem)
    for copy in (*in_copies, out_copy):
        copy.start()
    spread_rows(far_ref, far_spread_ref, width)

    meta = jnp.concatenate(
        [ref[:, pl.ds(width, META)].astype(jnp.float32) for ref in (here_ref, far_ref)], axis=0
    )
    ids, plan, gate = meta[:, 0:1], meta[:, 1:2], meta[:, 2:3]
    hot = ids == 2.0
    dest = jnp.where(hot, plan, ids)
    index_of = functools.partial(
        token_index, tok_rows=tok_rows, outer=outer, expert=expert, narrow=narrow
    )
    column_index = index_of(lax.broadcasted_iota(jnp.int32, (rows, rows), 0))
    row_index = index_of(lax.broadcasted_iota(jnp.int32, (rows, rows), 1))
    before = (row_index < column_index).astype(jnp.float32).astype(jnp.bfloat16)
    lane = lax.broadcasted_iota(jnp.int32, (rows, META), 1).astype(jnp.float32)
    onehot = (lane == dest).astype(jnp.float32)
    counts = jnp.dot(before, onehot.astype(jnp.bfloat16), preferred_element_type=jnp.float32)
    rank = jnp.sum(onehot * counts, axis=1, keepdims=True)
    at_home = dest == narrow.astype(jnp.float32)
    limit = jnp.where(at_home, meta[0:1, 3:4], meta[half : half + 1, 3:4])
    kept = rank < limit
    cold_rows = kept & at_home & jnp.logical_not(hot)
    hot_rows = kept & hot
    if not split_hot:
        hot_rows = hot_rows & at_home

    def hidden(weights, keep):
        tiles = weights.shape[0]
        group = hid_ref.shape[2] // LANE

        def pair(index, _):
            first = index * group
            total = jnp.zeros((2 * rows, group * LANE), jnp.float32)
            for step in range(2 * width // (2 * STEP)):
                depth = pl.ds(step * 2 * STEP, 2 * STEP)
                block = weights[first, depth, :]
                if group == 2:
                    block = jnp.concatenate([block, weights[first + 1, depth, :]], axis=1)
                spread = jnp.concatenate([near_spread_ref[:, depth], far_spread_ref[:, depth]], axis=0)
                total = total + jnp.dot(spread, block, preferred_element_type=jnp.float32)
            gate_in = jnp.concatenate([total[:half], total[rows : rows + half]], axis=0)
            up_in = jnp.concatenate([total[half:rows], total[rows + half :]], axis=0)
            value = jax.nn.silu(gate_in) * up_in
            if keep is not None:
                value = jnp.where(keep, value, 0.0)
            hid_ref[index] = value.astype(jnp.bfloat16)
            return 0

        lax.fori_loop(0, tiles // group, pair, 0)
        parts = [hid_ref[i] for i in range(tiles // group)]
        return parts[0] if len(parts) == 1 else jnp.concatenate(parts, axis=1)

    shared_hidden = hidden(shared_in, None)
    cold_hidden = hidden(cold_in, cold_rows)
    for copy in in_copies:
        copy.wait()
    hot_hidden = hidden(hot_in, hot_rows)
    out_copy.wait()
    def down(chunk, _):
        columns = pl.ds(pl.multiple_of(chunk * DOWN_CHUNK, DOWN_CHUNK), DOWN_CHUNK)
        routed = jnp.dot(cold_hidden, cold_out[:, columns], preferred_element_type=jnp.float32)
        routed = routed + jnp.dot(
            hot_hidden, hot_out[:, columns], preferred_element_type=jnp.float32
        )
        total = gate * routed + jnp.dot(
            shared_hidden, shared_out[:, columns], preferred_element_type=jnp.float32
        )
        mine_ref[:, columns] = total[:half]
        other_ref[:, columns] = total[half:].astype(jnp.bfloat16)
        return 0

    lax.fori_loop(0, width // DOWN_CHUNK, down, 0)


def layer(here, far, near_spread, weights, tok_rows):
    shared_in, cold_in, hot_in, shared_out, cold_out, hot_out = weights
    half = here.shape[0]
    width = here.shape[1] - META
    hot_part = hot_in.shape[2]
    split_hot = hot_part % (2 * LANE) == 0
    hot_used = hot_part // 2 if split_hot else hot_part
    in_vmem = pl.BlockSpec(memory_space=pltpu.VMEM)
    in_hbm = pl.BlockSpec(memory_space=pltpu.HBM)
    held = 8 * half * width + 6 * hot_used * width
    tiles = (shared_in.shape[0], cold_in.shape[0], hot_used // LANE)
    group = 2 if all(count % 2 == 0 for count in tiles) else 1
    most = max(tiles) // group
    return pl.pallas_call(
        functools.partial(layer_kernel, split_hot, tok_rows, lax.axis_size("expert")),
        out_shape=(
            pltpu.VMEM((half, width), jnp.float32),
            pltpu.VMEM((half, width), jnp.bfloat16),
        ),
        in_specs=[in_vmem] * 5 + [in_hbm] + [in_vmem] * 2 + [in_hbm],
        out_specs=(in_vmem, in_vmem),
        scratch_shapes=[
            pltpu.VMEM((2 * half, 2 * width), jnp.bfloat16),
            pltpu.VMEM((hot_used // LANE, 2 * width, LANE), jnp.bfloat16),
            pltpu.VMEM((hot_used, width), jnp.bfloat16),
            pltpu.SemaphoreType.DMA((hot_used // LANE,)),
            pltpu.SemaphoreType.DMA,
            pltpu.VMEM((most, 2 * half, LANE * group), jnp.bfloat16),
        ],
        compiler_params=pltpu.CompilerParams(vmem_limit_bytes=held + (4 << 20)),
        name="layer",
    )(
        here,
        far,
        pltpu.with_memory_space_constraint(near_spread, pltpu.VMEM),
        pltpu.with_memory_space_constraint(shared_in, pltpu.VMEM),
        pltpu.with_memory_space_constraint(cold_in, pltpu.VMEM),
        pltpu.with_memory_space_constraint(hot_in, pltpu.HBM),
        shared_out,
        cold_out,
        pltpu.with_memory_space_constraint(hot_out, pltpu.HBM),
    )


def body(
    tokens,
    expert_ids,
    replica_plan,
    route_gate,
    capacity,
    cold_gate_up,
    cold_down,
    hot_gate_up,
    hot_down,
    shared_gate_up,
    shared_down,
):
    tok_rows, width = tokens.shape
    outer = lax.axis_size("expert")
    high = outer // 2
    packed = pack(tokens, expert_ids, replica_plan, route_gate, capacity)
    shared_in, shared_held = fetch(shared_gate_up, packed)
    line = join(
        shared_held, [packed] + [expert_swap(packed, 2 * step) for step in range(1, high)]
    )
    cold_in, cold_held = fetch(cold_gate_up, line)
    here = join(cold_held, [line, expert_swap(line, 1)])
    near_spread = spread_near(here)
    far = narrow_swap(here)
    weights = (shared_in, cold_in, hot_gate_up, shared_down, cold_down[0], hot_down)
    mine, other = layer(here, far, near_spread, weights, tok_rows)
    mine = mine + narrow_swap(other).astype(jnp.float32)
    part = tok_rows * high
    mine = mine[:part] + expert_swap(mine[part:].astype(jnp.bfloat16), 1).astype(jnp.float32)
    total = mine[:tok_rows]
    for step in range(1, high):
        block = mine[step * tok_rows : (step + 1) * tok_rows].astype(jnp.bfloat16)
        total = total + expert_swap(block, 2 * step).astype(jnp.float32)
    return total.astype(jnp.bfloat16)


def solution(mesh):
    in_specs = (
        P(("groups", "expert", "narrow"), None),
        P(("groups", "expert", "narrow")),
        P(("groups", "expert", "narrow")),
        P(("groups", "expert", "narrow")),
        P(("groups", "narrow")),
        P("narrow", None, None, "expert"),
        P("narrow", "expert", None),
        P(None, None, "expert"),
        P("expert", None),
        P(None, None, ("expert", "narrow")),
        P(("expert", "narrow"), None),
    )
    out_specs = P(("groups", "expert", "narrow"), None)
    return jax.shard_map(body, mesh=mesh, in_specs=in_specs, out_specs=out_specs, check_vma=False)
```

```python
import functools

import jax
import jax.numpy as jnp
from jax import lax
from jax.experimental import pallas as pl
from jax.experimental.pallas import tpu as pltpu
from jax.sharding import PartitionSpec as P

META = 128
LANE = 128
STEP = 512
DOWN_CHUNK = 1280


def expert_swap(x, bits):
    size = lax.axis_size("expert")
    return lax.ppermute(x, "expert", [(i, i ^ bits) for i in range(size)])


def narrow_swap(x):
    return lax.ppermute(x, "narrow", [(0, 1), (1, 0)])


def token_index(row, tok_rows, outer, expert, narrow):
    block = row // tok_rows
    other_narrow = block // outer
    other_low = (block % outer) // (outer // 2)
    other_high = block % (outer // 2)
    from_expert = expert ^ (2 * other_high + other_low)
    from_narrow = narrow ^ other_narrow
    return (from_expert * 2 + from_narrow) * tok_rows + row % tok_rows


def pack_kernel(tokens_ref, ids_ref, plan_ref, gate_ref, capacity_ref, packed_ref):
    rows, width = tokens_ref.shape
    packed_ref[:, pl.ds(0, width)] = tokens_ref[...]
    own = lax.broadcasted_iota(jnp.int32, (rows, rows), 0) == lax.broadcasted_iota(
        jnp.int32, (rows, rows), 1
    )

    def per_row(ref):
        spread = jnp.broadcast_to(ref[...].astype(jnp.float32), (rows, rows))
        return jnp.sum(jnp.where(own, spread, 0.0), axis=1, keepdims=True)

    lane = lax.broadcasted_iota(jnp.int32, (rows, META), 1)
    meta = jnp.where(lane == 0, per_row(ids_ref), 0.0)
    meta = jnp.where(lane == 1, per_row(plan_ref), meta)
    meta = jnp.where(lane == 2, per_row(gate_ref), meta)
    meta = jnp.where(lane == 3, capacity_ref[...].astype(jnp.float32), meta)
    packed_ref[:, pl.ds(width, META)] = meta.astype(jnp.bfloat16)


def pack(tokens, ids, plan, gate, capacity):
    rows, width = tokens.shape
    return pl.pallas_call(
        pack_kernel,
        out_shape=pltpu.VMEM((rows, width + META), jnp.bfloat16),
        in_specs=[pl.BlockSpec(memory_space=pltpu.VMEM)] * 5,
        out_specs=pl.BlockSpec(memory_space=pltpu.VMEM),
        name="pack",
    )(tokens, *(v.reshape(1, -1) for v in (ids, plan, gate, capacity)))


def tile_copies(source, target, sems, base):
    width = source.shape[0]
    flat = source.reshape(2 * width, source.shape[2])
    copies = []
    for tile in range(target.shape[0]):
        start = base + tile * LANE
        if not isinstance(start, int):
            start = pl.multiple_of(start, LANE)
        copies.append(
            pltpu.make_async_copy(
                flat.at[:, pl.ds(start, LANE)], target.at[tile], sems.at[tile]
            )
        )
    return copies


def spread_rows(x_ref, spread_ref, width):
    rows = x_ref.shape[0]
    source_lane = lax.broadcasted_iota(jnp.int32, (LANE, 4 * LANE), 0)
    target_lane = lax.broadcasted_iota(jnp.int32, (LANE, 4 * LANE), 1)
    aim = jnp.where(target_lane < 2 * LANE, 2 * source_lane, 2 * source_lane + 1 + 2 * LANE)
    spread = (target_lane == aim).astype(jnp.float32).astype(jnp.bfloat16)
    for block in range(width // LANE):
        wide = jnp.dot(
            x_ref[:, pl.ds(block * LANE, LANE)], spread, preferred_element_type=jnp.float32
        ).astype(jnp.bfloat16)
        columns = pl.ds(block * 2 * LANE, 2 * LANE)
        spread_ref[pl.ds(0, rows), columns] = wide[:, : 2 * LANE]
        spread_ref[pl.ds(rows, rows), columns] = wide[:, 2 * LANE :]


def fetch_kernel(source_ref, after_ref, target_ref, done_ref, sems):
    del after_ref
    source = source_ref if len(source_ref.shape) == 3 else source_ref.at[0]
    copies = tile_copies(source, target_ref, sems, 0)
    for copy in copies:
        copy.start()
    for copy in copies:
        copy.wait()
    done_ref[...] = jnp.zeros_like(done_ref)


def join_kernel(*refs):
    pieces, joined_ref = refs[1:-1], refs[-1]
    joined_ref[...] = jnp.concatenate(
        [piece[...].astype(jnp.float32) for piece in pieces], axis=0
    ).astype(joined_ref.dtype)


def join(after, pieces):
    rows, width = pieces[0].shape
    in_vmem = pl.BlockSpec(memory_space=pltpu.VMEM)
    return pl.pallas_call(
        join_kernel,
        out_shape=pltpu.VMEM((len(pieces) * rows, width), pieces[0].dtype),
        in_specs=[in_vmem] * (1 + len(pieces)),
        out_specs=in_vmem,
        compiler_params=pltpu.CompilerParams(vmem_limit_bytes=4 << 20),
        name="join",
    )(after, *pieces)


def fetch(source, after):
    width, _, part = source.shape[-3:]
    size = source.size * source.dtype.itemsize
    return pl.pallas_call(
        fetch_kernel,
        out_shape=(
            pltpu.VMEM((part // LANE, 2 * width, LANE), jnp.bfloat16),
            pltpu.VMEM((8, LANE), jnp.float32),
        ),
        in_specs=[pl.BlockSpec(memory_space=pltpu.HBM), pl.BlockSpec(memory_space=pltpu.VMEM)],
        out_specs=(pl.BlockSpec(memory_space=pltpu.VMEM),) * 2,
        scratch_shapes=[pltpu.SemaphoreType.DMA((part // LANE,))],
        cost_estimate=pl.CostEstimate(flops=0, bytes_accessed=2 * size, transcendentals=0),
        compiler_params=pltpu.CompilerParams(vmem_limit_bytes=4 << 20),
        name="fetch",
    )(pltpu.with_memory_space_constraint(source, pltpu.HBM), after)


def near_spread_kernel(here_ref, spread_ref):
    spread_rows(here_ref, spread_ref, spread_ref.shape[1] // 2)


def spread_near(here):
    half, width = here.shape[0], here.shape[1] - META
    in_vmem = pl.BlockSpec(memory_space=pltpu.VMEM)
    return pl.pallas_call(
        near_spread_kernel,
        out_shape=pltpu.VMEM((2 * half, 2 * width), jnp.bfloat16),
        in_specs=[in_vmem],
        out_specs=in_vmem,
        compiler_params=pltpu.CompilerParams(vmem_limit_bytes=4 << 20),
        name="spread",
    )(here)


def layer_kernel(
    split_hot,
    tok_rows,
    outer,
    here_ref,
    far_ref,
    near_spread_ref,
    shared_in,
    cold_in,
    hot_in_ref,
    shared_out,
    cold_out,
    hot_out_ref,
    mine_ref,
    other_ref,
    shared_hidden_ref,
    cold_hidden_ref,
    hot_hidden_ref,
    gate_ref,
    hot_out,
    far_spread_ref,
    hot_in,
    in_sems,
    out_sem,
    hid_ref,
):
    width = here_ref.shape[1] - META
    narrow = lax.axis_index("narrow")
    expert = lax.axis_index("expert")
    half = here_ref.shape[0]
    rows = 2 * half
    hot_used = hot_out.shape[0]
    base = narrow * hot_used if split_hot else 0
    in_copies = tile_copies(hot_in_ref, hot_in, in_sems, base)
    taken = hot_out_ref
    if split_hot:
        taken = hot_out_ref.at[pl.ds(pl.multiple_of(base, LANE), hot_used)]
    out_copy = pltpu.make_async_copy(taken, hot_out, out_sem)
    for copy in (*in_copies, out_copy):
        copy.start()
    spread_rows(far_ref, far_spread_ref, width)

    meta = jnp.concatenate(
        [ref[:, pl.ds(width, META)].astype(jnp.float32) for ref in (here_ref, far_ref)], axis=0
    )
    ids, plan, gate = meta[:, 0:1], meta[:, 1:2], meta[:, 2:3]
    hot = ids == 2.0
    dest = jnp.where(hot, plan, ids)
    index_of = functools.partial(
        token_index, tok_rows=tok_rows, outer=outer, expert=expert, narrow=narrow
    )
    column_index = index_of(lax.broadcasted_iota(jnp.int32, (rows, rows), 0))
    row_index = index_of(lax.broadcasted_iota(jnp.int32, (rows, rows), 1))
    before = (row_index < column_index).astype(jnp.float32).astype(jnp.bfloat16)
    lane = lax.broadcasted_iota(jnp.int32, (rows, META), 1).astype(jnp.float32)
    onehot = (lane == dest).astype(jnp.float32)
    counts = jnp.dot(before, onehot.astype(jnp.bfloat16), preferred_element_type=jnp.float32)
    rank = jnp.sum(onehot * counts, axis=1, keepdims=True)
    at_home = dest == narrow.astype(jnp.float32)
    limit = jnp.where(at_home, meta[0:1, 3:4], meta[half : half + 1, 3:4])
    kept = rank < limit
    cold_rows = kept & at_home & jnp.logical_not(hot)
    hot_rows = kept & hot
    if not split_hot:
        hot_rows = hot_rows & at_home

    def hidden(weights, keep):
        tiles = weights.shape[0]
        group = hid_ref.shape[2] // LANE

        def pair(index, _):
            first = index * group
            total = jnp.zeros((2 * rows, group * LANE), jnp.float32)
            for step in range(2 * width // (2 * STEP)):
                depth = pl.ds(step * 2 * STEP, 2 * STEP)
                block = weights[first, depth, :]
                if group == 2:
                    block = jnp.concatenate([block, weights[first + 1, depth, :]], axis=1)
                spread = jnp.concatenate([near_spread_ref[:, depth], far_spread_ref[:, depth]], axis=0)
                total = total + jnp.dot(spread, block, preferred_element_type=jnp.float32)
            gate_in = jnp.concatenate([total[:half], total[rows : rows + half]], axis=0)
            up_in = jnp.concatenate([total[half:rows], total[rows + half :]], axis=0)
            value = jax.nn.silu(gate_in) * up_in
            if keep is not None:
                value = jnp.where(keep, value, 0.0)
            hid_ref[index] = value.astype(jnp.bfloat16)
            return 0

        lax.fori_loop(0, tiles // group, pair, 0)
        parts = [hid_ref[i] for i in range(tiles // group)]
        return parts[0] if len(parts) == 1 else jnp.concatenate(parts, axis=1)

    gate_ref[...] = jnp.broadcast_to(gate, gate_ref.shape)
    shared_hidden_ref[...] = hidden(shared_in, None)
    cold_hidden_ref[...] = hidden(cold_in, cold_rows)
    for copy in in_copies:
        copy.wait()
    hot_hidden_ref[...] = hidden(hot_in, hot_rows)
    out_copy.wait()
    down_columns(
        0,
        (shared_hidden_ref, cold_hidden_ref, hot_hidden_ref),
        gate_ref,
        (shared_out, cold_out, hot_out),
        mine_ref,
        other_ref,
    )


def down_columns(first, hiddens, gate_ref, weights, mine_ref, other_ref):
    half, width = mine_ref.shape
    shared_hidden, cold_hidden, hot_hidden = (ref[...] for ref in hiddens)
    shared_out, cold_out, hot_out = weights
    gate = gate_ref[:, 0:1]

    def down(chunk, _):
        columns = pl.ds(pl.multiple_of(first + chunk * DOWN_CHUNK, DOWN_CHUNK), DOWN_CHUNK)
        stored = pl.ds(pl.multiple_of(chunk * DOWN_CHUNK, DOWN_CHUNK), DOWN_CHUNK)
        routed = jnp.dot(cold_hidden, cold_out[:, columns], preferred_element_type=jnp.float32)
        routed = routed + jnp.dot(
            hot_hidden, hot_out[:, columns], preferred_element_type=jnp.float32
        )
        total = gate * routed + jnp.dot(
            shared_hidden, shared_out[:, columns], preferred_element_type=jnp.float32
        )
        mine_ref[:, stored] = total[:half]
        other_ref[:, stored] = total[half:].astype(jnp.bfloat16)
        return 0

    lax.fori_loop(0, width // DOWN_CHUNK, down, 0)


def rest_kernel(
    shared_hidden,
    cold_hidden,
    hot_hidden,
    gate_ref,
    shared_out,
    cold_out,
    hot_out,
    mine_ref,
    other_ref,
):
    down_columns(
        shared_out.shape[1] - mine_ref.shape[1],
        (shared_hidden, cold_hidden, hot_hidden),
        gate_ref,
        (shared_out, cold_out, hot_out),
        mine_ref,
        other_ref,
    )


def rest(hiddens, gate, weights):
    half = gate.shape[0] // 2
    columns = weights[0].shape[1] // 2
    in_vmem = pl.BlockSpec(memory_space=pltpu.VMEM)
    fixed = [pltpu.with_memory_space_constraint(w, pltpu.VMEM) for w in (*hiddens, gate)]
    return pl.pallas_call(
        rest_kernel,
        out_shape=(
            pltpu.VMEM((half, columns), jnp.float32),
            pltpu.VMEM((half, columns), jnp.bfloat16),
        ),
        in_specs=[in_vmem] * 7,
        out_specs=(in_vmem, in_vmem),
        compiler_params=pltpu.CompilerParams(vmem_limit_bytes=4 << 20),
        name="rest",
    )(*fixed, weights[0], weights[1], pltpu.with_memory_space_constraint(weights[2], pltpu.VMEM))


def layer(here, far, near_spread, weights, tok_rows):
    shared_in, cold_in, hot_in, shared_out, cold_out, hot_out = weights
    half = here.shape[0]
    width = here.shape[1] - META
    hot_part = hot_in.shape[2]
    split_hot = hot_part % (2 * LANE) == 0
    hot_used = hot_part // 2 if split_hot else hot_part
    in_vmem = pl.BlockSpec(memory_space=pltpu.VMEM)
    in_hbm = pl.BlockSpec(memory_space=pltpu.HBM)
    held = 8 * half * width + 4 * hot_used * width
    tiles = (shared_in.shape[0], cold_in.shape[0], hot_used // LANE)
    group = 2 if all(count % 2 == 0 for count in tiles) else 1
    most = max(tiles) // group
    return pl.pallas_call(
        functools.partial(layer_kernel, split_hot, tok_rows, lax.axis_size("expert")),
        out_shape=(
            pltpu.VMEM((half, width // 2), jnp.float32),
            pltpu.VMEM((half, width // 2), jnp.bfloat16),
            *(pltpu.VMEM((2 * half, count * LANE), jnp.bfloat16) for count in tiles),
            pltpu.VMEM((2 * half, LANE), jnp.float32),
            pltpu.VMEM((hot_used, width), jnp.bfloat16),
        ),
        in_specs=[in_vmem] * 5 + [in_hbm] + [in_vmem] * 2 + [in_hbm],
        out_specs=(in_vmem,) * 7,
        scratch_shapes=[
            pltpu.VMEM((2 * half, 2 * width), jnp.bfloat16),
            pltpu.VMEM((hot_used // LANE, 2 * width, LANE), jnp.bfloat16),
            pltpu.SemaphoreType.DMA((hot_used // LANE,)),
            pltpu.SemaphoreType.DMA,
            pltpu.VMEM((most, 2 * half, LANE * group), jnp.bfloat16),
        ],
        compiler_params=pltpu.CompilerParams(vmem_limit_bytes=held + (4 << 20)),
        name="layer",
    )(
        here,
        far,
        pltpu.with_memory_space_constraint(near_spread, pltpu.VMEM),
        pltpu.with_memory_space_constraint(shared_in, pltpu.VMEM),
        pltpu.with_memory_space_constraint(cold_in, pltpu.VMEM),
        pltpu.with_memory_space_constraint(hot_in, pltpu.HBM),
        shared_out,
        cold_out,
        pltpu.with_memory_space_constraint(hot_out, pltpu.HBM),
    )


def body(
    tokens,
    expert_ids,
    replica_plan,
    route_gate,
    capacity,
    cold_gate_up,
    cold_down,
    hot_gate_up,
    hot_down,
    shared_gate_up,
    shared_down,
):
    tok_rows, width = tokens.shape
    outer = lax.axis_size("expert")
    high = outer // 2
    packed = pack(tokens, expert_ids, replica_plan, route_gate, capacity)
    shared_in, shared_held = fetch(shared_gate_up, packed)
    line = join(
        shared_held, [packed] + [expert_swap(packed, 2 * step) for step in range(1, high)]
    )
    cold_in, cold_held = fetch(cold_gate_up, line)
    here = join(cold_held, [line, expert_swap(line, 1)])
    near_spread = spread_near(here)
    far = narrow_swap(here)
    weights = (shared_in, cold_in, hot_gate_up, shared_down, cold_down[0], hot_down)
    first, first_other, *hiddens, gate, hot_out = layer(here, far, near_spread, weights, tok_rows)
    second, second_other = rest(hiddens, gate, (shared_down, cold_down[0], hot_out))
    part = tok_rows * high
    halves = []
    for mine, other in ((first, first_other), (second, second_other)):
        mine = mine + narrow_swap(other).astype(jnp.float32)
        low = expert_swap(mine[part:].astype(jnp.bfloat16), 1)
        halves.append(mine[:part] + low.astype(jnp.float32))
    mine = jnp.concatenate(halves, axis=1)
    total = mine[:tok_rows]
    for step in range(1, high):
        block = mine[step * tok_rows : (step + 1) * tok_rows].astype(jnp.bfloat16)
        total = total + expert_swap(block, 2 * step).astype(jnp.float32)
    return total.astype(jnp.bfloat16)


def solution(mesh):
    in_specs = (
        P(("groups", "expert", "narrow"), None),
        P(("groups", "expert", "narrow")),
        P(("groups", "expert", "narrow")),
        P(("groups", "expert", "narrow")),
        P(("groups", "narrow")),
        P("narrow", None, None, "expert"),
        P("narrow", "expert", None),
        P(None, None, "expert"),
        P("expert", None),
        P(None, None, ("expert", "narrow")),
        P(("expert", "narrow"), None),
    )
    out_specs = P(("groups", "expert", "narrow"), None)
    return jax.shard_map(body, mesh=mesh, in_specs=in_specs, out_specs=out_specs, check_vma=False)
```

```python
import functools

import jax
import jax.numpy as jnp
from jax import lax
from jax.experimental import pallas as pl
from jax.experimental.pallas import tpu as pltpu
from jax.sharding import PartitionSpec as P

META = 128
LANE = 128
STEP = 512
DOWN_CHUNK = 1280


def expert_swap(x, bits):
    size = lax.axis_size("expert")
    return lax.ppermute(x, "expert", [(i, i ^ bits) for i in range(size)])


def narrow_swap(x):
    return lax.ppermute(x, "narrow", [(0, 1), (1, 0)])


def token_index(row, tok_rows, outer, expert, narrow):
    block = row // tok_rows
    other_narrow = block // outer
    other_low = (block % outer) // (outer // 2)
    other_high = block % (outer // 2)
    from_expert = expert ^ (2 * other_high + other_low)
    from_narrow = narrow ^ other_narrow
    return (from_expert * 2 + from_narrow) * tok_rows + row % tok_rows


def pack_kernel(tokens_ref, ids_ref, plan_ref, gate_ref, capacity_ref, packed_ref):
    rows, width = tokens_ref.shape
    packed_ref[:, pl.ds(0, width)] = tokens_ref[...]
    own = lax.broadcasted_iota(jnp.int32, (rows, rows), 0) == lax.broadcasted_iota(
        jnp.int32, (rows, rows), 1
    )

    def per_row(ref):
        spread = jnp.broadcast_to(ref[...].astype(jnp.float32), (rows, rows))
        return jnp.sum(jnp.where(own, spread, 0.0), axis=1, keepdims=True)

    lane = lax.broadcasted_iota(jnp.int32, (rows, META), 1)
    meta = jnp.where(lane == 0, per_row(ids_ref), 0.0)
    meta = jnp.where(lane == 1, per_row(plan_ref), meta)
    meta = jnp.where(lane == 2, per_row(gate_ref), meta)
    meta = jnp.where(lane == 3, capacity_ref[...].astype(jnp.float32), meta)
    packed_ref[:, pl.ds(width, META)] = meta.astype(jnp.bfloat16)


def pack(tokens, ids, plan, gate, capacity):
    rows, width = tokens.shape
    return pl.pallas_call(
        pack_kernel,
        out_shape=pltpu.VMEM((rows, width + META), jnp.bfloat16),
        in_specs=[pl.BlockSpec(memory_space=pltpu.VMEM)] * 5,
        out_specs=pl.BlockSpec(memory_space=pltpu.VMEM),
        name="pack",
    )(tokens, *(v.reshape(1, -1) for v in (ids, plan, gate, capacity)))


def tile_copies(source, target, sems, base):
    width = source.shape[0]
    flat = source.reshape(2 * width, source.shape[2])
    copies = []
    for tile in range(target.shape[0]):
        start = base + tile * LANE
        if not isinstance(start, int):
            start = pl.multiple_of(start, LANE)
        copies.append(
            pltpu.make_async_copy(
                flat.at[:, pl.ds(start, LANE)], target.at[tile], sems.at[tile]
            )
        )
    return copies


def spread_rows(x_ref, spread_ref, width):
    rows = x_ref.shape[0]
    source_lane = lax.broadcasted_iota(jnp.int32, (LANE, 4 * LANE), 0)
    target_lane = lax.broadcasted_iota(jnp.int32, (LANE, 4 * LANE), 1)
    aim = jnp.where(target_lane < 2 * LANE, 2 * source_lane, 2 * source_lane + 1 + 2 * LANE)
    spread = (target_lane == aim).astype(jnp.float32).astype(jnp.bfloat16)
    for block in range(width // LANE):
        wide = jnp.dot(
            x_ref[:, pl.ds(block * LANE, LANE)], spread, preferred_element_type=jnp.float32
        ).astype(jnp.bfloat16)
        columns = pl.ds(block * 2 * LANE, 2 * LANE)
        spread_ref[pl.ds(0, rows), columns] = wide[:, : 2 * LANE]
        spread_ref[pl.ds(rows, rows), columns] = wide[:, 2 * LANE :]


def fetch_kernel(source_ref, after_ref, target_ref, done_ref, sems):
    del after_ref
    source = source_ref if len(source_ref.shape) == 3 else source_ref.at[0]
    copies = tile_copies(source, target_ref, sems, 0)
    for copy in copies:
        copy.start()
    for copy in copies:
        copy.wait()
    done_ref[...] = jnp.zeros_like(done_ref)


def join_kernel(*refs):
    pieces, joined_ref = refs[1:-1], refs[-1]
    joined_ref[...] = jnp.concatenate(
        [piece[...].astype(jnp.float32) for piece in pieces], axis=0
    ).astype(joined_ref.dtype)


def join(after, pieces):
    rows, width = pieces[0].shape
    in_vmem = pl.BlockSpec(memory_space=pltpu.VMEM)
    return pl.pallas_call(
        join_kernel,
        out_shape=pltpu.VMEM((len(pieces) * rows, width), pieces[0].dtype),
        in_specs=[in_vmem] * (1 + len(pieces)),
        out_specs=in_vmem,
        compiler_params=pltpu.CompilerParams(vmem_limit_bytes=4 << 20),
        name="join",
    )(after, *pieces)


def fetch(source, after):
    width, _, part = source.shape[-3:]
    size = source.size * source.dtype.itemsize
    return pl.pallas_call(
        fetch_kernel,
        out_shape=(
            pltpu.VMEM((part // LANE, 2 * width, LANE), jnp.bfloat16),
            pltpu.VMEM((8, LANE), jnp.float32),
        ),
        in_specs=[pl.BlockSpec(memory_space=pltpu.HBM), pl.BlockSpec(memory_space=pltpu.VMEM)],
        out_specs=(pl.BlockSpec(memory_space=pltpu.VMEM),) * 2,
        scratch_shapes=[pltpu.SemaphoreType.DMA((part // LANE,))],
        cost_estimate=pl.CostEstimate(flops=0, bytes_accessed=2 * size, transcendentals=0),
        compiler_params=pltpu.CompilerParams(vmem_limit_bytes=4 << 20),
        name="fetch",
    )(pltpu.with_memory_space_constraint(source, pltpu.HBM), after)


def near_spread_kernel(here_ref, spread_ref):
    spread_rows(here_ref, spread_ref, spread_ref.shape[1] // 2)


def spread_near(here):
    half, width = here.shape[0], here.shape[1] - META
    in_vmem = pl.BlockSpec(memory_space=pltpu.VMEM)
    return pl.pallas_call(
        near_spread_kernel,
        out_shape=pltpu.VMEM((2 * half, 2 * width), jnp.bfloat16),
        in_specs=[in_vmem],
        out_specs=in_vmem,
        compiler_params=pltpu.CompilerParams(vmem_limit_bytes=4 << 20),
        name="spread",
    )(here)


def layer_kernel(
    split_hot,
    tok_rows,
    outer,
    here_ref,
    far_ref,
    near_spread_ref,
    shared_in,
    cold_in,
    hot_in_ref,
    shared_out,
    cold_out,
    hot_out_ref,
    mine_ref,
    other_ref,
    shared_hidden_ref,
    cold_hidden_ref,
    hot_hidden_ref,
    gate_ref,
    hot_out,
    far_spread_ref,
    hot_in,
    in_sems,
    out_sem,
    hid_ref,
):
    width = here_ref.shape[1] - META
    narrow = lax.axis_index("narrow")
    expert = lax.axis_index("expert")
    half = here_ref.shape[0]
    rows = 2 * half
    hot_used = hot_out.shape[0]
    base = narrow * hot_used if split_hot else 0
    in_copies = tile_copies(hot_in_ref, hot_in, in_sems, base)
    taken = hot_out_ref
    if split_hot:
        taken = hot_out_ref.at[pl.ds(pl.multiple_of(base, LANE), hot_used)]
    out_copy = pltpu.make_async_copy(taken, hot_out, out_sem)
    for copy in (*in_copies, out_copy):
        copy.start()
    spread_rows(far_ref, far_spread_ref, width)

    meta = jnp.concatenate(
        [ref[:, pl.ds(width, META)].astype(jnp.float32) for ref in (here_ref, far_ref)], axis=0
    )
    ids, plan, gate = meta[:, 0:1], meta[:, 1:2], meta[:, 2:3]
    hot = ids == 2.0
    dest = jnp.where(hot, plan, ids)
    index_of = functools.partial(
        token_index, tok_rows=tok_rows, outer=outer, expert=expert, narrow=narrow
    )
    column_index = index_of(lax.broadcasted_iota(jnp.int32, (rows, rows), 0))
    row_index = index_of(lax.broadcasted_iota(jnp.int32, (rows, rows), 1))
    before = (row_index < column_index).astype(jnp.float32).astype(jnp.bfloat16)
    lane = lax.broadcasted_iota(jnp.int32, (rows, META), 1).astype(jnp.float32)
    onehot = (lane == dest).astype(jnp.float32)
    counts = jnp.dot(before, onehot.astype(jnp.bfloat16), preferred_element_type=jnp.float32)
    rank = jnp.sum(onehot * counts, axis=1, keepdims=True)
    at_home = dest == narrow.astype(jnp.float32)
    limit = jnp.where(at_home, meta[0:1, 3:4], meta[half : half + 1, 3:4])
    kept = rank < limit
    cold_rows = kept & at_home & jnp.logical_not(hot)
    hot_rows = kept & hot
    if not split_hot:
        hot_rows = hot_rows & at_home

    def hidden(weights, keep):
        tiles = weights.shape[0]
        group = hid_ref.shape[2] // LANE

        def pair(index, _):
            first = index * group
            total = jnp.zeros((2 * rows, group * LANE), jnp.float32)
            for step in range(2 * width // (2 * STEP)):
                depth = pl.ds(step * 2 * STEP, 2 * STEP)
                block = weights[first, depth, :]
                if group == 2:
                    block = jnp.concatenate([block, weights[first + 1, depth, :]], axis=1)
                spread = jnp.concatenate([near_spread_ref[:, depth], far_spread_ref[:, depth]], axis=0)
                total = total + jnp.dot(spread, block, preferred_element_type=jnp.float32)
            gate_in = jnp.concatenate([total[:half], total[rows : rows + half]], axis=0)
            up_in = jnp.concatenate([total[half:rows], total[rows + half :]], axis=0)
            value = jax.nn.silu(gate_in) * up_in
            if keep is not None:
                value = jnp.where(keep, value, 0.0)
            hid_ref[index] = value.astype(jnp.bfloat16)
            return 0

        lax.fori_loop(0, tiles // group, pair, 0)
        parts = [hid_ref[i] for i in range(tiles // group)]
        return parts[0] if len(parts) == 1 else jnp.concatenate(parts, axis=1)

    gate_ref[...] = jnp.broadcast_to(gate, gate_ref.shape)
    shared_hidden_ref[...] = hidden(shared_in, None)
    cold_hidden_ref[...] = hidden(cold_in, cold_rows)
    for copy in in_copies:
        copy.wait()
    hot_hidden_ref[...] = hidden(hot_in, hot_rows)
    out_copy.wait()
    down_columns(
        0,
        (shared_hidden_ref, cold_hidden_ref, hot_hidden_ref),
        gate_ref,
        (shared_out, cold_out, hot_out),
        mine_ref,
        other_ref,
    )


def down_columns(first, hiddens, gate_ref, weights, mine_ref, other_ref, size=DOWN_CHUNK):
    half, width = mine_ref.shape
    shared_hidden, cold_hidden, hot_hidden = (ref[...] for ref in hiddens)
    shared_out, cold_out, hot_out = weights
    gate = gate_ref[:, 0:1]

    def down(chunk, _):
        columns = pl.ds(pl.multiple_of(first + chunk * size, size), size)
        stored = pl.ds(pl.multiple_of(chunk * size, size), size)
        routed = jnp.dot(cold_hidden, cold_out[:, columns], preferred_element_type=jnp.float32)
        routed = routed + jnp.dot(
            hot_hidden, hot_out[:, columns], preferred_element_type=jnp.float32
        )
        total = gate * routed + jnp.dot(
            shared_hidden, shared_out[:, columns], preferred_element_type=jnp.float32
        )
        mine_ref[:, stored] = total[:half]
        other_ref[:, stored] = total[half:].astype(jnp.bfloat16)
        return 0

    lax.fori_loop(0, width // size, down, 0)


def rest_kernel(
    shared_hidden,
    cold_hidden,
    hot_hidden,
    gate_ref,
    shared_out,
    cold_out,
    hot_out,
    mine_ref,
    other_ref,
):
    down_columns(
        shared_out.shape[1] - mine_ref.shape[1],
        (shared_hidden, cold_hidden, hot_hidden),
        gate_ref,
        (shared_out, cold_out, hot_out),
        mine_ref,
        other_ref,
        mine_ref.shape[1],
    )


def rest(hiddens, gate, weights):
    half = gate.shape[0] // 2
    columns = weights[0].shape[1] // 2
    in_vmem = pl.BlockSpec(memory_space=pltpu.VMEM)
    fixed = [pltpu.with_memory_space_constraint(w, pltpu.VMEM) for w in (*hiddens, gate)]
    return pl.pallas_call(
        rest_kernel,
        out_shape=(
            pltpu.VMEM((half, columns), jnp.float32),
            pltpu.VMEM((half, columns), jnp.bfloat16),
        ),
        in_specs=[in_vmem] * 7,
        out_specs=(in_vmem, in_vmem),
        compiler_params=pltpu.CompilerParams(vmem_limit_bytes=4 << 20),
        name="rest",
    )(*fixed, weights[0], weights[1], pltpu.with_memory_space_constraint(weights[2], pltpu.VMEM))


def layer(here, far, near_spread, weights, tok_rows):
    shared_in, cold_in, hot_in, shared_out, cold_out, hot_out = weights
    half = here.shape[0]
    width = here.shape[1] - META
    hot_part = hot_in.shape[2]
    split_hot = hot_part % (2 * LANE) == 0
    hot_used = hot_part // 2 if split_hot else hot_part
    in_vmem = pl.BlockSpec(memory_space=pltpu.VMEM)
    in_hbm = pl.BlockSpec(memory_space=pltpu.HBM)
    held = 8 * half * width + 4 * hot_used * width
    tiles = (shared_in.shape[0], cold_in.shape[0], hot_used // LANE)
    group = 2 if all(count % 2 == 0 for count in tiles) else 1
    most = max(tiles) // group
    return pl.pallas_call(
        functools.partial(layer_kernel, split_hot, tok_rows, lax.axis_size("expert")),
        out_shape=(
            pltpu.VMEM((half, width // 2), jnp.float32),
            pltpu.VMEM((half, width // 2), jnp.bfloat16),
            *(pltpu.VMEM((2 * half, count * LANE), jnp.bfloat16) for count in tiles),
            pltpu.VMEM((2 * half, LANE), jnp.float32),
            pltpu.VMEM((hot_used, width), jnp.bfloat16),
        ),
        in_specs=[in_vmem] * 5 + [in_hbm] + [in_vmem] * 2 + [in_hbm],
        out_specs=(in_vmem,) * 7,
        scratch_shapes=[
            pltpu.VMEM((2 * half, 2 * width), jnp.bfloat16),
            pltpu.VMEM((hot_used // LANE, 2 * width, LANE), jnp.bfloat16),
            pltpu.SemaphoreType.DMA((hot_used // LANE,)),
            pltpu.SemaphoreType.DMA,
            pltpu.VMEM((most, 2 * half, LANE * group), jnp.bfloat16),
        ],
        compiler_params=pltpu.CompilerParams(vmem_limit_bytes=held + (4 << 20)),
        name="layer",
    )(
        here,
        far,
        pltpu.with_memory_space_constraint(near_spread, pltpu.VMEM),
        pltpu.with_memory_space_constraint(shared_in, pltpu.VMEM),
        pltpu.with_memory_space_constraint(cold_in, pltpu.VMEM),
        pltpu.with_memory_space_constraint(hot_in, pltpu.HBM),
        shared_out,
        cold_out,
        pltpu.with_memory_space_constraint(hot_out, pltpu.HBM),
    )


def body(
    tokens,
    expert_ids,
    replica_plan,
    route_gate,
    capacity,
    cold_gate_up,
    cold_down,
    hot_gate_up,
    hot_down,
    shared_gate_up,
    shared_down,
):
    tok_rows, width = tokens.shape
    outer = lax.axis_size("expert")
    high = outer // 2
    packed = pack(tokens, expert_ids, replica_plan, route_gate, capacity)
    shared_in, shared_held = fetch(shared_gate_up, packed)
    line = join(
        shared_held, [packed] + [expert_swap(packed, 2 * step) for step in range(1, high)]
    )
    cold_in, cold_held = fetch(cold_gate_up, line)
    here = join(cold_held, [line, expert_swap(line, 1)])
    near_spread = spread_near(here)
    far = narrow_swap(here)
    weights = (shared_in, cold_in, hot_gate_up, shared_down, cold_down[0], hot_down)
    first, first_other, *hiddens, gate, hot_out = layer(here, far, near_spread, weights, tok_rows)
    second, second_other = rest(hiddens, gate, (shared_down, cold_down[0], hot_out))
    part = tok_rows * high
    halves = []
    for mine, other in ((first, first_other), (second, second_other)):
        mine = mine + narrow_swap(other).astype(jnp.float32)
        low = expert_swap(mine[part:].astype(jnp.bfloat16), 1)
        halves.append(mine[:part] + low.astype(jnp.float32))
    mine = jnp.concatenate(halves, axis=1)
    total = mine[:tok_rows]
    for step in range(1, high):
        block = mine[step * tok_rows : (step + 1) * tok_rows].astype(jnp.bfloat16)
        total = total + expert_swap(block, 2 * step).astype(jnp.float32)
    return total.astype(jnp.bfloat16)


def solution(mesh):
    in_specs = (
        P(("groups", "expert", "narrow"), None),
        P(("groups", "expert", "narrow")),
        P(("groups", "expert", "narrow")),
        P(("groups", "expert", "narrow")),
        P(("groups", "narrow")),
        P("narrow", None, None, "expert"),
        P("narrow", "expert", None),
        P(None, None, "expert"),
        P("expert", None),
        P(None, None, ("expert", "narrow")),
        P(("expert", "narrow"), None),
    )
    out_specs = P(("groups", "expert", "narrow"), None)
    return jax.shard_map(body, mesh=mesh, in_specs=in_specs, out_specs=out_specs, check_vma=False)
```
